32 devices in a mesh: gz: 4 (over y, x), xy: 8 (over z, core).
Axes of the slice: x: 2, y: 2, z: 4, core: 2. Of those that a mesh axis runs over, the one named last changes fastest.
Arguments:
- u_wind: bfloat16 [4, 2048, 2048], P('gz', 'xy'), may hold values from -6 to 6
- v_wind: bfloat16 [4, 2048, 2048], P('gz', 'xy'), may hold values from -6 to 6
- w_wind: bfloat16 [4, 2048, 2048], P('gz', 'xy'), may hold values from -4 to 4
- scalar: bfloat16 [4, 2048, 2048], P('gz', 'xy'), may hold values from -6 to 6
- heights: int32 [2048, 2048], P('xy'), may hold values from 0 to 4
- wall_class: int32 [2048, 2048], P('xy'), may hold values from 0 to 7
- wall_area: float32 [8], replicated, may hold values from 0.1 to 2
- wall_heat: float32 [8], replicated, may hold values from 0.1 to 1
Outputs:
- tendency: bfloat16 [4, 2048, 2048], P('gz', 'xy')
- pressure: float32 [4, 2048, 2048], P('gz', 'xy')
The draws below stay inside these ranges and needn't reach their ends.
Inputs may be any that keep to these rules, and one draw needn't show every extreme that they name: A cell of level l lies in the building layer of its column where l < heights. `wall_class`: class index of each column into wall_area and wall_heat.
All inputs are finite; a program needn't handle non-finite values.
Results may differ from the reference program's by a relative error of at most 0.0039.
Values may be sent and summed in bfloat16 or wider, within the bound.
A program may use at most 192 MiB of HBM per device.

```python
import math
import jax
import jax.numpy as jnp
from jax import lax

NX = 2048
NY = 2048
NCLASS = 8
NZ = 4
KX = 640
KY = 640
BAND = 64


def set_ends(drawn, own_key, least, largest):
    longest = drawn.shape.index(max(drawn.shape))
    spots = []
    for shift in (0, 1):
        where = [jax.random.randint(jax.random.fold_in(own_key, axis), (), 0, length) for axis, length in enumerate(drawn.shape)]
        where[longest] = (where[longest] + shift) % drawn.shape[longest]
        spots.append(tuple(where))
    return drawn.at[spots[0]].set(least).at[spots[1]].set(largest)


def steps_of(key, dims, split, least, top_value):
    gain = 1.0
    for dim, shards_of in split:
        draws = jax.random.uniform(jax.random.fold_in(jax.random.fold_in(key, 6), dim), (shards_of,), jnp.float32, least / len(split), top_value / len(split))
        gain = gain * jnp.repeat(jnp.exp(draws), dims[dim] // shards_of).reshape((-1,) + (1,) * (len(dims) - 1 - dim))
    return gain


def normal_values(stream_key, extent, deviation, limit, cuts=(), held_as=jnp.bfloat16):
    result = jax.random.normal(stream_key, extent, jnp.float32) * deviation
    if len(cuts) > 0:
        result = steps_of(stream_key, extent, cuts, -0.22, 0.18) * result
    return jnp.clip(result, min=-limit, max=limit).astype(held_as)


def setup_inputs(seed: int = 0) -> dict:
    splits = jax.random.split(jax.random.key(seed), 9)
    u_wind = normal_values(splits[0], (NZ, NX, NY), 1.0, 6.0, ((0, 4), (1, 8)))
    v_wind = normal_values(splits[1], (NZ, NX, NY), 1.0, 6.0, ((0, 4), (1, 8)))
    w_wind = normal_values(splits[2], (NZ, NX, NY), 0.5, 4.0, ((0, 4), (1, 8)))
    scalar = normal_values(splits[3], (NZ, NX, NY), 1.0, 6.0, ((0, 4), (1, 8)))
    heights = set_ends(jax.random.randint(splits[4], (NX, NY), 0, NZ + 1), jax.random.fold_in(splits[4], 1), 0, NZ).astype(jnp.int32)
    wall_class = set_ends(jax.random.randint(splits[5], (NX, NY), 0, NCLASS), jax.random.fold_in(splits[5], 1), 0, NCLASS - 1).astype(jnp.int32)
    wall_area = jnp.clip(jnp.exp(jax.random.uniform(splits[6], (NCLASS,), jnp.float32, math.log(0.1), math.log(2.0))), 0.1, 2.0)
    wall_heat = jnp.clip(jnp.exp(jax.random.uniform(splits[7], (NCLASS,), jnp.float32, math.log(0.1), math.log(1.0))), 0.1, 1.0)
    return {"u_wind": u_wind, "v_wind": v_wind, "w_wind": w_wind, "scalar": scalar, "heights": heights, "wall_class": wall_class, "wall_area": wall_area, "wall_heat": wall_heat}


GRID_STEP = 2.5
LEVEL_STEP = 2.5
DRAG_STEP = 0.5
GUST_FLOOR = 0.25

def signed_index(count, positions):
    return jnp.where(positions < count // 2, positions, positions - count)

def wave_number(count, positions):
    return 2.0 * math.pi / (count * GRID_STEP) * positions.astype(jnp.float32)

def reference(u_wind, v_wind, w_wind, scalar, heights, wall_class, wall_area, wall_heat):
    levels = jnp.arange(NZ, dtype=jnp.int32)
    inside = (levels[:, None, None] < heights[None]).astype(jnp.float32)
    wall_density = wall_area[wall_class]
    wall_source = wall_heat[wall_class]
    east_wind = u_wind.astype(jnp.float32)
    north_wind = v_wind.astype(jnp.float32)
    vertical_wind = w_wind.astype(jnp.float32)
    tracer = scalar.astype(jnp.float32)
    wind_speed = jnp.sqrt(east_wind * east_wind + north_wind * north_wind + GUST_FLOOR)
    drag_factor = 1.0 + DRAG_STEP * wall_density[None] * inside * wind_speed
    east_star = east_wind / drag_factor
    north_star = north_wind / drag_factor
    zero_plane = jnp.zeros((1, NX, NY), jnp.float32)
    w_above = jnp.concatenate([vertical_wind[1:], zero_plane], axis=0)
    c_above = jnp.concatenate([tracer[1:], zero_plane], axis=0)
    c_below = jnp.concatenate([zero_plane, tracer[:-1]], axis=0)
    vertical = (w_above * (c_above + tracer) * 0.5 - vertical_wind * (tracer + c_below) * 0.5) / LEVEL_STEP
    stretch = (w_above - vertical_wind) / LEVEL_STEP
    row_signed = signed_index(NX, jnp.arange(NX, dtype=jnp.int32))
    column_signed = signed_index(NY, jnp.arange(NY, dtype=jnp.int32))
    wave_x = wave_number(NX, row_signed)
    wave_y = wave_number(NY, column_signed)
    keep = ((row_signed >= -KX) & (row_signed < KX))[:, None] & ((column_signed >= -KY) & (column_signed < KY))[None, :]
    band_rows = jnp.concatenate([jnp.arange(BAND, dtype=jnp.int32), jnp.arange(NX - BAND, NX, dtype=jnp.int32)])

    def horizontal(members):
        east_hat = jnp.fft.fft2(members[0])
        north_hat = jnp.fft.fft2(members[1])
        flux_east = jnp.fft.fft2(members[2])
        flux_north = jnp.fft.fft2(members[3])
        stretch_hat = jnp.fft.fft2(members[4])
        derive_x = 1j * wave_x[:, None]
        derive_y = 1j * wave_y[None, :]
        rhs_hat = jnp.where(keep, derive_x * east_hat + derive_y * north_hat + stretch_hat, 0.0)
        div_hat = jnp.where(keep, derive_x * flux_east + derive_y * flux_north, 0.0)
        return (jnp.real(jnp.fft.ifft2(div_hat)), rhs_hat[band_rows])
    divergence, rhs_band = lax.map(horizontal, (east_star, north_star, east_star * tracer, north_star * tracer, stretch))
    coupling = 1.0 / (LEVEL_STEP * LEVEL_STEP)
    wave_band = wave_x[band_rows]
    diagonal = -2.0 * coupling - (wave_band[:, None] ** 2 + wave_y[None, :] ** 2)
    upper_ratio = jnp.zeros_like(diagonal)
    reduced = jnp.zeros_like(rhs_band[0])
    ratios = []
    reduced_list = []
    for level_index in range(NZ):
        pivot_value = diagonal - coupling * upper_ratio
        upper_ratio = coupling / pivot_value
        reduced = (rhs_band[level_index] - coupling * reduced) / pivot_value
        ratios.append(upper_ratio)
        reduced_list.append(reduced)
    solved_value = jnp.zeros_like(reduced)
    solved_list = [None] * NZ
    for level_index in reversed(range(NZ)):
        solved_value = reduced_list[level_index] - ratios[level_index] * solved_value
        solved_list[level_index] = solved_value
    solved = jnp.stack(solved_list)

    def expand(band_modes):
        spectrum = jnp.zeros((NX, NY), band_modes.dtype).at[band_rows].set(band_modes)
        return jnp.real(jnp.fft.ifft2(spectrum))
    pressure = lax.map(expand, solved).astype(jnp.float32)
    tendency = (-divergence - vertical + wall_source[None] * inside).astype(jnp.bfloat16)
    return (tendency, pressure)
```

```python
from functools import partial
import math

import jax
import jax.numpy as jnp
import ml_dtypes
import numpy as np
from jax import lax
from jax.sharding import PartitionSpec as P

KX = 640
KY = 640
BAND = 64

GRID_STEP = 2.5
LEVEL_STEP = 2.5
DRAG_STEP = 0.5
GUST_FLOOR = 0.25

BF = jnp.bfloat16
F32 = jnp.float32


def round_up(value, unit):
    return -(-value // unit) * unit


def split_np(table):
    high = table.astype(ml_dtypes.bfloat16)
    low = (table - high.astype(np.float64)).astype(ml_dtypes.bfloat16)
    return high, low


def split(array):
    high = lax.reduce_precision(array, exponent_bits=8, mantissa_bits=7)
    return high.astype(BF), (array - high).astype(BF)


def mode_rows(modes_c, modes_s, count):
    t = np.arange(count)
    cos_rows = np.cos(2.0 * np.pi / count * (np.outer(modes_c, t) % count))
    sin_rows = np.sin(2.0 * np.pi / count * (np.outer(modes_s, t) % count))
    return cos_rows, sin_rows


def y_layout(strips, count):
    half = KY // strips
    share = round_up(2 * half + 2, 8)
    table = np.zeros((strips, share, count))
    synth = np.zeros((strips, share))
    wave = np.zeros((strips, share))
    for d in range(strips):
        modes = np.arange(d * half, (d + 1) * half)
        table[d, :half], table[d, half : 2 * half] = mode_rows(modes, modes, count)
        wave[d, :half] = wave[d, half : 2 * half] = modes
        synth[d, : 2 * half] = 2.0 / count
    synth[0, 0] = 1.0 / count
    ends = np.array([KY])
    cos_end, sin_end = mode_rows(ends, ends, count)
    table[-1, 2 * half], table[-1, 2 * half + 1] = cos_end[0], sin_end[0]
    wave[-1, 2 * half : 2 * half + 2] = KY
    synth[-1, 2 * half : 2 * half + 2] = 1.0 / count
    wave *= 2.0 * np.pi / (count * GRID_STEP)
    return half, share, table.reshape(strips * share, count), wave, synth


def x_band(count):
    width = round_up(2 * BAND + 2, 8)
    modes = np.arange(BAND)
    basis = np.zeros((width, count))
    basis[:BAND], basis[BAND : 2 * BAND] = mode_rows(modes, modes, count)
    ends = np.array([BAND])
    cos_end, sin_end = mode_rows(ends, ends, count)
    basis[2 * BAND], basis[2 * BAND + 1] = cos_end[0], sin_end[0]
    unit = 2.0 * np.pi / (count * GRID_STEP)
    wave = np.zeros(width)
    wave[:BAND] = wave[BAND : 2 * BAND] = modes * unit
    wave[2 * BAND : 2 * BAND + 2] = BAND * unit
    slope = np.zeros((width, count))
    slope[:BAND] = wave[:BAND, None] * basis[BAND : 2 * BAND]
    slope[BAND : 2 * BAND] = -wave[:BAND, None] * basis[:BAND]
    slope[2 * BAND] = wave[2 * BAND] * basis[2 * BAND + 1]
    slope[2 * BAND + 1] = -wave[2 * BAND] * basis[2 * BAND]
    synth = np.zeros(width)
    synth[: 2 * BAND] = 2.0 / count
    synth[0] = 1.0 / count
    synth[2 * BAND : 2 * BAND + 2] = 1.0 / count
    return width, basis, slope, wave, synth


def x_operators(count):
    modes = np.arange(1, KX)
    unit = 2.0 * np.pi / (count * GRID_STEP)
    lag = np.arange(count)
    angle = 2.0 * np.pi / count * (np.outer(modes, lag) % count)
    end_angle = 2.0 * np.pi / count * (KX * lag % count)
    slope = -(2.0 * (modes * unit) @ np.sin(angle) + KX * unit * np.sin(end_angle)) / count
    keep = (1.0 + 2.0 * np.cos(angle).sum(axis=0) + np.cos(end_angle)) / count
    shift = (lag[None, :] - lag[:, None]) % count
    ends = 2.0 * np.pi / count * (KX * lag % count)
    return slope[shift], keep[shift], np.cos(ends), np.sin(ends), KX * unit


def swap_scaled(array, half, wave):
    cos_part = array[..., :half, :]
    sin_part = array[..., half : 2 * half, :]
    cos_end = array[..., 2 * half : 2 * half + 1, :]
    sin_end = array[..., 2 * half + 1 : 2 * half + 2, :]
    rest = array[..., 2 * half + 2 :, :]
    swapped = jnp.concatenate([sin_part, -cos_part, sin_end, -cos_end, rest], axis=-2)
    return swapped * wave


def dot(a, b, dims):
    return lax.dot_general(a, b, (dims, ((), ())), preferred_element_type=F32)


def per_device(tables, u_wind, v_wind, w_wind, scalar, heights, wall_class, wall_area, wall_heat):
    _, row_count, column_count = u_wind.shape
    strips = lax.axis_size("xy")
    groups = lax.axis_size("gz")
    level = lax.axis_index("gz")
    strip = lax.axis_index("xy")
    half, share, width = tables["half"], tables["share"], tables["width"]
    count_x = row_count * strips

    w_flat, c_flat = w_wind[0], scalar[0]
    up = [(i, i + 1) for i in range(groups - 1)]
    down = [(i + 1, i) for i in range(groups - 1)]
    c_below = lax.ppermute(c_flat, "gz", up)

    inside = level < heights
    density = jnp.zeros(heights.shape, F32)
    heat = jnp.zeros(heights.shape, F32)
    for k in range(wall_area.shape[0]):
        match = wall_class == k
        density = jnp.where(match, wall_area[k], density)
        heat = jnp.where(match, wall_heat[k], heat)
    east, north = u_wind[0].astype(F32), v_wind[0].astype(F32)
    tracer = c_flat.astype(F32)
    speed = jnp.sqrt(east * east + north * north + GUST_FLOOR)
    drag = 1.0 + jnp.where(inside, DRAG_STEP * density * speed, 0.0)
    east_star = east / drag
    north_star = north / drag
    heating = jnp.where(inside, heat, 0.0)

    first_row = strip * row_count
    rows = lambda t: lax.dynamic_slice_in_dim(t, first_row, row_count, 1)
    basis = jnp.concatenate([rows(tables["basis"][0]), rows(tables["basis"][1])], axis=1)
    slope = jnp.concatenate([rows(tables["slope"][0]), rows(tables["slope"][1])], axis=1)
    mn = ((1,), (0,))

    def low_modes(table, field):
        high, low = split(field)
        return dot(table, jnp.concatenate([high, high], axis=0), mn) + dot(
            table[:, :row_count], low, mn
        )

    w_modes = dot(basis, jnp.concatenate([w_flat, w_flat], axis=0), mn) * (1.0 / LEVEL_STEP)
    a_modes = low_modes(slope, east_star) - w_modes
    b_modes = low_modes(basis, north_star)
    modes_high, modes_low = split(jnp.concatenate([a_modes, w_modes, b_modes], axis=0))
    fields = jnp.concatenate(
        [
            (east_star * tracer).astype(BF),
            (north_star * tracer).astype(BF),
            modes_high,
            modes_low,
        ],
        axis=0,
    )
    y_high, y_low = tables["y"]
    nt = ((1,), (1,))
    spectra = dot(y_high, fields, nt)
    low = dot(y_low, modes_high, nt)
    spectra = spectra.reshape(strips, share, -1)
    low = low.reshape(strips, share, -1)
    first = 2 * row_count
    press = spectra[..., first : first + 3 * width] + spectra[..., first + 3 * width :] + low
    wave_y = jnp.asarray(tables["wave_y"], F32)[..., None]
    flux_v = swap_scaled(spectra[..., row_count : 2 * row_count], half, wave_y)
    rhs_part = press[..., :width] + swap_scaled(press[..., 2 * width :], half, wave_y)
    sent = jnp.concatenate(
        [spectra[..., :row_count], flux_v, rhs_part, press[..., width : 2 * width]], axis=-1
    ).astype(BF)
    got = lax.all_to_all(sent, "xy", split_axis=0, concat_axis=0, tiled=True)

    flux = w_flat.astype(F32) * (tracer + c_below.astype(F32)) * (0.5 / LEVEL_STEP)
    flux_above = lax.ppermute(flux.astype(BF), "gz", down)

    sums = jnp.sum(got[..., 2 * row_count :].astype(F32), axis=0)
    all_sums = lax.all_gather(sums, "gz", axis=0, tiled=False)
    wave_own = lax.dynamic_index_in_dim(
        jnp.asarray(tables["wave_y"], F32), strip, 0, keepdims=False
    )
    wave_x = jnp.asarray(tables["wave_x"], F32)
    coupling = 1.0 / (LEVEL_STEP * LEVEL_STEP)
    diagonal = -2.0 * coupling - (wave_x * wave_x)[None, :] - (wave_own * wave_own)[:, None]
    ratio = jnp.zeros_like(diagonal)
    reduced = jnp.zeros_like(diagonal)
    ratios, reduced_list = [], []
    for l in range(groups):
        rhs = all_sums[l, :, :width]
        if l + 1 < groups:
            rhs = rhs + all_sums[l + 1, :, width:]
        inverse = 1.0 / (diagonal - coupling * ratio)
        ratio = coupling * inverse
        reduced = (rhs - coupling * reduced) * inverse
        ratios.append(ratio)
        reduced_list.append(reduced)
    value = jnp.zeros_like(diagonal)
    own = jnp.zeros_like(diagonal)
    for l in reversed(range(groups)):
        value = reduced_list[l] - ratios[l] * value
        own = jnp.where(level == l, value, own)
    corner = own[2 * half : 2 * half + 2, 2 * BAND : 2 * BAND + 2]
    sign = np.array([[-1.0, 1.0], [1.0, -1.0]], np.float32)
    fixed = corner + sign * corner[::-1, ::-1]
    corner = jnp.where(strip == strips - 1, fixed, corner)
    own = lax.dynamic_update_slice(own, corner, (2 * half, 2 * BAND))
    synth_y = lax.dynamic_index_in_dim(
        jnp.asarray(tables["synth_y"], F32), strip, 0, keepdims=False
    )[:, None]
    own = own * (synth_y * jnp.asarray(tables["synth_x"], F32)[None, :] * tables["gain"])

    z_east = jnp.swapaxes(got[..., :row_count], 0, 1).reshape(share, count_x)
    z_north = jnp.swapaxes(got[..., row_count : 2 * row_count], 0, 1).reshape(share, count_x)
    both = jnp.concatenate([z_east, z_north], axis=1)
    product = dot(both, tables["x_high"], mn)
    if tables["x_low"] is not None:
        product = product + dot(both, tables["x_low"], mn)
    ends = jnp.asarray(tables["ends"], F32)
    pair = both[2 * half : 2 * half + 2].astype(F32)
    pe, pn = pair[:, :count_x], pair[:, count_x:]
    top = tables["top"]
    ec, es = jnp.sum(pe * ends[0], axis=1), jnp.sum(pe * ends[1], axis=1)
    nc, ns = jnp.sum(pn * ends[0], axis=1), jnp.sum(pn * ends[1], axis=1)
    cos_gain = (-top * ec + ns) / count_x
    sin_gain = (-top * es - nc) / count_x
    imag = cos_gain[:, None] * ends[0] + sin_gain[:, None] * ends[1]
    imag = jnp.where(strip == strips - 1, jnp.stack([-imag[1], imag[0]]), 0.0)
    product = lax.dynamic_update_slice(
        product, product[2 * half : 2 * half + 2] + imag, (2 * half, 0)
    )
    product = product * synth_y
    back = jnp.swapaxes(product.reshape(share, strips, row_count), 0, 1).astype(BF)
    own = jnp.broadcast_to(own.astype(BF)[None], (strips, share, width))
    returned = lax.all_to_all(
        jnp.concatenate([back, own], axis=-1), "xy", split_axis=0, concat_axis=0, tiled=True
    ).reshape(strips * share, row_count + width)

    tn = ((0,), (0,))
    planes = dot(returned, y_high, tn)
    if tables["low_back"]:
        planes = planes + dot(returned, y_low, tn)
        pressed = planes[row_count:]
    else:
        pressed = planes[row_count:] + dot(returned[:, row_count:], y_low, tn)
    p_high, p_low = split(pressed)
    b_high, b_low = rows(tables["basis"][0]), rows(tables["basis"][1])
    pressure = dot(
        jnp.concatenate([b_high, b_low, b_high], axis=0),
        jnp.concatenate([p_high, p_high, p_low], axis=0),
        tn,
    ) * (1.0 / tables["gain"])
    vertical = flux_above.astype(F32) - flux
    tendency = (heating - planes[:row_count] - vertical).astype(BF)
    return (tendency[None], pressure[None])


OPTIONS = {"low_back": False, "x_low": False}


def solution(mesh):

    def whole(u_wind, *others):
        _, count_x, count_y = u_wind.shape
        strips = mesh.shape["xy"]
        half, share, y_table, wave_y, synth_y = y_layout(strips, count_y)
        width, basis, slope, wave_x, synth_x = x_band(count_x)
        x_slope, x_keep, end_cos, end_sin, top = x_operators(count_x)
        x_high, x_low = split_np(np.concatenate([x_slope, x_keep], axis=0))
        tables = {
            "half": half,
            "share": share,
            "width": width,
            "y": split_np(y_table),
            "wave_y": wave_y,
            "synth_y": synth_y,
            "basis": split_np(basis),
            "slope": split_np(slope),
            "wave_x": wave_x,
            "synth_x": synth_x,
            "gain": float(count_x),
            "x_high": x_high,
            "x_low": x_low if OPTIONS["x_low"] else None,
            "ends": np.stack([end_cos, end_sin]),
            "top": top,
            "low_back": OPTIONS["low_back"],
        }
        return jax.shard_map(
            partial(per_device, tables),
            mesh=mesh,
            in_specs=(P("gz", "xy", None),) * 4 + (P("xy", None),) * 2 + (P(), P()),
            out_specs=(P("gz", "xy", None), P("gz", "xy", None)),
            check_vma=False,
        )(u_wind, *others)

    return whole
```

```python
from functools import partial
import math

import jax
import jax.numpy as jnp
import ml_dtypes
import numpy as np
from jax import lax
from jax.experimental import pallas as pl
from jax.experimental.pallas import tpu as pltpu
from jax.sharding import PartitionSpec as P

KX = 640
KY = 640
BAND = 64

GRID_STEP = 2.5
LEVEL_STEP = 2.5
DRAG_STEP = 0.5
GUST_FLOOR = 0.25

BF = jnp.bfloat16
F32 = jnp.float32


def round_up(value, unit):
    return -(-value // unit) * unit


def split_np(table):
    high = table.astype(ml_dtypes.bfloat16)
    low = (table - high.astype(np.float64)).astype(ml_dtypes.bfloat16)
    return high, low


def split(array):
    high = lax.reduce_precision(array, exponent_bits=8, mantissa_bits=7)
    return high.astype(BF), (array - high).astype(BF)


def mode_rows(modes_c, modes_s, count):
    t = np.arange(count)
    cos_rows = np.cos(2.0 * np.pi / count * (np.outer(modes_c, t) % count))
    sin_rows = np.sin(2.0 * np.pi / count * (np.outer(modes_s, t) % count))
    return cos_rows, sin_rows


def y_layout(strips, count):
    half = KY // strips
    share = round_up(2 * half + 2, 8)
    table = np.zeros((strips, share, count))
    synth = np.zeros((strips, share))
    wave = np.zeros((strips, share))
    for d in range(strips):
        modes = np.arange(d * half, (d + 1) * half)
        table[d, :half], table[d, half : 2 * half] = mode_rows(modes, modes, count)
        wave[d, :half] = wave[d, half : 2 * half] = modes
        synth[d, : 2 * half] = 2.0 / count
    synth[0, 0] = 1.0 / count
    ends = np.array([KY])
    cos_end, sin_end = mode_rows(ends, ends, count)
    table[-1, 2 * half], table[-1, 2 * half + 1] = cos_end[0], sin_end[0]
    wave[-1, 2 * half : 2 * half + 2] = KY
    synth[-1, 2 * half : 2 * half + 2] = 1.0 / count
    wave *= 2.0 * np.pi / (count * GRID_STEP)
    slope = np.zeros((strips, share, count))
    slope[:, :half] = wave[:, :half, None] * table[:, half : 2 * half]
    slope[:, half : 2 * half] = -wave[:, half : 2 * half, None] * table[:, :half]
    slope[:, 2 * half] = wave[:, 2 * half, None] * table[:, 2 * half + 1]
    slope[:, 2 * half + 1] = -wave[:, 2 * half + 1, None] * table[:, 2 * half]
    flat = (strips * share, count)
    return half, share, table.reshape(flat), slope.reshape(flat), wave, synth


def x_band(count):
    width = round_up(2 * BAND + 2, 8)
    modes = np.arange(BAND)
    basis = np.zeros((width, count))
    basis[:BAND], basis[BAND : 2 * BAND] = mode_rows(modes, modes, count)
    ends = np.array([BAND])
    cos_end, sin_end = mode_rows(ends, ends, count)
    basis[2 * BAND], basis[2 * BAND + 1] = cos_end[0], sin_end[0]
    unit = 2.0 * np.pi / (count * GRID_STEP)
    wave = np.zeros(width)
    wave[:BAND] = wave[BAND : 2 * BAND] = modes * unit
    wave[2 * BAND : 2 * BAND + 2] = BAND * unit
    slope = np.zeros((width, count))
    slope[:BAND] = wave[:BAND, None] * basis[BAND : 2 * BAND]
    slope[BAND : 2 * BAND] = -wave[:BAND, None] * basis[:BAND]
    slope[2 * BAND] = wave[2 * BAND] * basis[2 * BAND + 1]
    slope[2 * BAND + 1] = -wave[2 * BAND] * basis[2 * BAND]
    synth = np.zeros(width)
    synth[: 2 * BAND] = 2.0 / count
    synth[0] = 1.0 / count
    synth[2 * BAND : 2 * BAND + 2] = 1.0 / count
    return width, basis, slope, wave, synth


def x_operators(count):
    modes = np.arange(1, KX)
    unit = 2.0 * np.pi / (count * GRID_STEP)
    lag = np.arange(count)
    angle = 2.0 * np.pi / count * (np.outer(modes, lag) % count)
    end_angle = 2.0 * np.pi / count * (KX * lag % count)
    slope = -(2.0 * (modes * unit) @ np.sin(angle) + KX * unit * np.sin(end_angle)) / count
    keep = (1.0 + 2.0 * np.cos(angle).sum(axis=0) + np.cos(end_angle)) / count
    shift = (lag[None, :] - lag[:, None]) % count
    ends = 2.0 * np.pi / count * (KX * lag % count)
    return slope[shift], keep[shift], np.cos(ends), np.sin(ends), KX * unit


def dot(a, b, dims):
    return lax.dot_general(a, b, (dims, ((), ())), preferred_element_type=F32)


def drag_kernel(level, area, wall_heat, u, v, c, heights, classes, fu, fv, us, vs, heating):
    rows, columns = u.shape
    lanes = min(512, columns)
    for r in range(0, rows, 16):
        for q in range(0, columns, lanes):
            at = (slice(r, r + 16), slice(q, q + lanes))
            kind = classes[at]
            density = jnp.full(kind.shape, area[0], F32)
            heat = jnp.full(kind.shape, wall_heat[0], F32)
            for k in range(1, area.shape[0]):
                match = kind == k
                density = jnp.where(match, area[k], density)
                heat = jnp.where(match, wall_heat[k], heat)
            inside = level[0] < heights[at]
            east, north = u[at].astype(F32), v[at].astype(F32)
            tracer = c[at].astype(F32)
            speed = jnp.sqrt(east * east + north * north + GUST_FLOOR)
            drag = 1.0 + jnp.where(inside, DRAG_STEP * density * speed, 0.0)
            inverse = 1.0 / drag
            east, north = east * inverse, north * inverse
            fu[at] = (east * tracer).astype(BF)
            fv[at] = (north * tracer).astype(BF)
            us[at] = east.astype(BF)
            vs[at] = north.astype(BF)
            heating[at] = jnp.where(inside, heat, 0.0)


def drag_fields(level, area, wall_heat, u, v, c, heights, classes):
    rows, columns = u.shape
    block = min(64, rows)
    small = pl.BlockSpec(memory_space=pltpu.SMEM)
    strip = pl.BlockSpec((block, columns), lambda i: (i, 0))
    shape = lambda dtype: jax.ShapeDtypeStruct((rows, columns), dtype)
    return pl.pallas_call(
        drag_kernel,
        grid=(rows // block,),
        in_specs=[small] * 3 + [strip] * 5,
        out_specs=[strip] * 5,
        out_shape=[shape(BF)] * 4 + [shape(F32)],
        compiler_params=pltpu.CompilerParams(vmem_limit_bytes=40 * 2**20),
        cost_estimate=pl.CostEstimate(
            flops=60 * rows * columns, bytes_accessed=26 * rows * columns, transcendentals=0
        ),
    )(level, area, wall_heat, u, v, c, heights, classes)


def per_device(tables, u_wind, v_wind, w_wind, scalar, heights, wall_class, wall_area, wall_heat):
    _, row_count, column_count = u_wind.shape
    strips = lax.axis_size("xy")
    groups = lax.axis_size("gz")
    level = lax.axis_index("gz")
    strip = lax.axis_index("xy")
    half, share, width = tables["half"], tables["share"], tables["width"]
    count_x = row_count * strips

    w_flat, c_flat = w_wind[0], scalar[0]
    up = [(i, i + 1) for i in range(groups - 1)]
    down = [(i + 1, i) for i in range(groups - 1)]
    c_below = lax.ppermute(c_flat, "gz", up)
    flux_u, flux_v, u_bf, v_bf, heating = drag_fields(
        level.reshape(1), wall_area, wall_heat, u_wind[0], v_wind[0], c_flat, heights, wall_class
    )

    mn, nt, tn = ((1,), (0,)), ((1,), (1,)), ((0,), (0,))
    y_high, y_low = tables["y"]
    s_high, s_low = tables["y_slope"]
    exchange = partial(lax.all_to_all, axis_name="xy", split_axis=0, concat_axis=0, tiled=True)
    blocks = lambda t: t.reshape(strips, share, -1).astype(BF)
    z_east = exchange(blocks(dot(y_high, flux_u, nt)))

    first_row = strip * row_count
    rows = lambda t: lax.dynamic_slice_in_dim(t, first_row, row_count, 1)
    basis = jnp.concatenate([rows(tables["basis"][0]), rows(tables["basis"][1])], axis=1)
    slope = jnp.concatenate([rows(tables["slope"][0]), rows(tables["slope"][1])], axis=1)
    low_modes = lambda table, field: dot(table, jnp.concatenate([field, field], axis=0), mn)
    w_modes = low_modes(basis, w_flat) * (1.0 / LEVEL_STEP)
    a_modes = low_modes(slope, u_bf) - w_modes
    b_modes = low_modes(basis, v_bf)

    def three(high, low, modes):
        m_high, m_low = split(modes)
        return dot(high, m_high, nt) + dot(high, m_low, nt) + dot(low, m_high, nt)

    rhs_part = three(y_high, y_low, a_modes) + three(s_high, s_low, b_modes)
    low_part = three(y_high, y_low, w_modes)
    got = exchange(blocks(jnp.concatenate([rhs_part, low_part], axis=1)))
    z_north = exchange(blocks(dot(s_high, flux_v, nt)))

    tracer = c_flat.astype(F32)
    flux = w_flat.astype(F32) * (tracer + c_below.astype(F32)) * (0.5 / LEVEL_STEP)
    flux_above = lax.ppermute(flux.astype(BF), "gz", down)

    sums = jnp.sum(got.astype(F32), axis=0)
    all_sums = lax.all_gather(sums, "gz", axis=0, tiled=False)
    wave_own = lax.dynamic_index_in_dim(
        jnp.asarray(tables["wave_y"], F32), strip, 0, keepdims=False
    )
    wave_x = jnp.asarray(tables["wave_x"], F32)
    coupling = 1.0 / (LEVEL_STEP * LEVEL_STEP)
    diagonal = -2.0 * coupling - (wave_x * wave_x)[None, :] - (wave_own * wave_own)[:, None]
    ratio = jnp.zeros_like(diagonal)
    reduced = jnp.zeros_like(diagonal)
    ratios, reduced_list = [], []
    for l in range(groups):
        rhs = all_sums[l, :, :width]
        if l + 1 < groups:
            rhs = rhs + all_sums[l + 1, :, width:]
        inverse = 1.0 / (diagonal - coupling * ratio)
        ratio = coupling * inverse
        reduced = (rhs - coupling * reduced) * inverse
        ratios.append(ratio)
        reduced_list.append(reduced)
    value = jnp.zeros_like(diagonal)
    own = jnp.zeros_like(diagonal)
    for l in reversed(range(groups)):
        value = reduced_list[l] - ratios[l] * value
        own = jnp.where(level == l, value, own)
    corner = own[2 * half : 2 * half + 2, 2 * BAND : 2 * BAND + 2]
    sign = np.array([[-1.0, 1.0], [1.0, -1.0]], np.float32)
    fixed = corner + sign * corner[::-1, ::-1]
    corner = jnp.where(strip == strips - 1, fixed, corner)
    own = lax.dynamic_update_slice(own, corner, (2 * half, 2 * BAND))
    synth_y = lax.dynamic_index_in_dim(
        jnp.asarray(tables["synth_y"], F32), strip, 0, keepdims=False
    )[:, None]
    own = own * (synth_y * jnp.asarray(tables["synth_x"], F32)[None, :] * tables["gain"])

    wide = lambda t: jnp.swapaxes(t, 0, 1).reshape(share, count_x)
    z_east, z_north = wide(z_east), wide(z_north)
    product = dot(z_east, tables["x_slope"], mn) + dot(z_north, tables["x_keep"], mn)
    ends = jnp.asarray(tables["ends"], F32)
    pe = z_east[2 * half : 2 * half + 2].astype(F32)
    pn = z_north[2 * half : 2 * half + 2].astype(F32)
    top = tables["top"]
    ec, es = jnp.sum(pe * ends[0], axis=1), jnp.sum(pe * ends[1], axis=1)
    nc, ns = jnp.sum(pn * ends[0], axis=1), jnp.sum(pn * ends[1], axis=1)
    cos_gain = (-top * ec + ns) / count_x
    sin_gain = (-top * es - nc) / count_x
    imag = cos_gain[:, None] * ends[0] + sin_gain[:, None] * ends[1]
    imag = jnp.where(strip == strips - 1, jnp.stack([-imag[1], imag[0]]), 0.0)
    product = lax.dynamic_update_slice(
        product, product[2 * half : 2 * half + 2] + imag, (2 * half, 0)
    )
    product = product * synth_y
    back = jnp.swapaxes(product.reshape(share, strips, row_count), 0, 1).astype(BF)
    returned = exchange(back).reshape(strips * share, row_count)
    solved = lax.all_gather(own.astype(BF), "xy", axis=0, tiled=True)

    pressed = dot(solved, y_high, tn) + dot(solved, y_low, tn)
    p_high, p_low = split(pressed)
    b_high, b_low = rows(tables["basis"][0]), rows(tables["basis"][1])
    pressure = dot(
        jnp.concatenate([b_high, b_low, b_high], axis=0),
        jnp.concatenate([p_high, p_high, p_low], axis=0),
        tn,
    ) * (1.0 / tables["gain"])
    vertical = flux_above.astype(F32) - flux
    tendency = (heating - dot(returned, y_high, tn) - vertical).astype(BF)
    return (tendency[None], pressure[None])


def solution(mesh):

    def whole(u_wind, *others):
        _, count_x, count_y = u_wind.shape
        strips = mesh.shape["xy"]
        half, share, y_table, y_slope, wave_y, synth_y = y_layout(strips, count_y)
        width, basis, slope, wave_x, synth_x = x_band(count_x)
        x_slope, x_keep, end_cos, end_sin, top = x_operators(count_x)
        tables = {
            "half": half,
            "share": share,
            "width": width,
            "y": split_np(y_table),
            "y_slope": split_np(y_slope),
            "wave_y": wave_y,
            "synth_y": synth_y,
            "basis": split_np(basis),
            "slope": split_np(slope),
            "wave_x": wave_x,
            "synth_x": synth_x,
            "gain": float(count_x),
            "x_slope": x_slope.astype(ml_dtypes.bfloat16),
            "x_keep": x_keep.astype(ml_dtypes.bfloat16),
            "ends": np.stack([end_cos, end_sin]),
            "top": top,
        }
        return jax.shard_map(
            partial(per_device, tables),
            mesh=mesh,
            in_specs=(P("gz", "xy", None),) * 4 + (P("xy", None),) * 2 + (P(), P()),
            out_specs=(P("gz", "xy", None), P("gz", "xy", None)),
            check_vma=False,
        )(u_wind, *others)

    return whole
```

```python
from functools import partial
import math

import jax
import jax.numpy as jnp
import ml_dtypes
import numpy as np
from jax import lax
from jax.experimental import pallas as pl
from jax.experimental.pallas import tpu as pltpu
from jax.sharding import PartitionSpec as P

KX = 640
KY = 640
BAND = 64

GRID_STEP = 2.5
LEVEL_STEP = 2.5
DRAG_STEP = 0.5
GUST_FLOOR = 0.25

BF = jnp.bfloat16
F32 = jnp.float32


def round_up(value, unit):
    return -(-value // unit) * unit


def split_np(table):
    high = table.astype(ml_dtypes.bfloat16)
    low = (table - high.astype(np.float64)).astype(ml_dtypes.bfloat16)
    return high, low


def split(array):
    high = lax.reduce_precision(array, exponent_bits=8, mantissa_bits=7)
    return high.astype(BF), (array - high).astype(BF)


def mode_rows(modes_c, modes_s, count):
    t = np.arange(count)
    cos_rows = np.cos(2.0 * np.pi / count * (np.outer(modes_c, t) % count))
    sin_rows = np.sin(2.0 * np.pi / count * (np.outer(modes_s, t) % count))
    return cos_rows, sin_rows


def y_layout(strips, count):
    half = KY // strips
    share = round_up(2 * half + 2, 8)
    table = np.zeros((strips, share, count))
    synth = np.zeros((strips, share))
    wave = np.zeros((strips, share))
    for d in range(strips):
        modes = np.arange(d * half, (d + 1) * half)
        table[d, :half], table[d, half : 2 * half] = mode_rows(modes, modes, count)
        wave[d, :half] = wave[d, half : 2 * half] = modes
        synth[d, : 2 * half] = 2.0 / count
    synth[0, 0] = 1.0 / count
    ends = np.array([KY])
    cos_end, sin_end = mode_rows(ends, ends, count)
    table[-1, 2 * half], table[-1, 2 * half + 1] = cos_end[0], sin_end[0]
    wave[-1, 2 * half : 2 * half + 2] = KY
    synth[-1, 2 * half : 2 * half + 2] = 1.0 / count
    wave *= 2.0 * np.pi / (count * GRID_STEP)
    slope = np.zeros((strips, share, count))
    slope[:, :half] = wave[:, :half, None] * table[:, half : 2 * half]
    slope[:, half : 2 * half] = -wave[:, half : 2 * half, None] * table[:, :half]
    slope[:, 2 * half] = wave[:, 2 * half, None] * table[:, 2 * half + 1]
    slope[:, 2 * half + 1] = -wave[:, 2 * half + 1, None] * table[:, 2 * half]
    flat = (strips * share, count)
    return half, share, table.reshape(flat), slope.reshape(flat), wave, synth


def x_band(count):
    width = round_up(2 * BAND + 2, 8)
    modes = np.arange(BAND)
    basis = np.zeros((width, count))
    basis[:BAND], basis[BAND : 2 * BAND] = mode_rows(modes, modes, count)
    ends = np.array([BAND])
    cos_end, sin_end = mode_rows(ends, ends, count)
    basis[2 * BAND], basis[2 * BAND + 1] = cos_end[0], sin_end[0]
    unit = 2.0 * np.pi / (count * GRID_STEP)
    wave = np.zeros(width)
    wave[:BAND] = wave[BAND : 2 * BAND] = modes * unit
    wave[2 * BAND : 2 * BAND + 2] = BAND * unit
    slope = np.zeros((width, count))
    slope[:BAND] = wave[:BAND, None] * basis[BAND : 2 * BAND]
    slope[BAND : 2 * BAND] = -wave[:BAND, None] * basis[:BAND]
    slope[2 * BAND] = wave[2 * BAND] * basis[2 * BAND + 1]
    slope[2 * BAND + 1] = -wave[2 * BAND] * basis[2 * BAND]
    synth = np.zeros(width)
    synth[: 2 * BAND] = 2.0 / count
    synth[0] = 1.0 / count
    synth[2 * BAND : 2 * BAND + 2] = 1.0 / count
    return width, basis, slope, wave, synth


def x_operators(count):
    modes = np.arange(1, KX)
    unit = 2.0 * np.pi / (count * GRID_STEP)
    lag = np.arange(count)
    angle = 2.0 * np.pi / count * (np.outer(modes, lag) % count)
    end_angle = 2.0 * np.pi / count * (KX * lag % count)
    slope = -(2.0 * (modes * unit) @ np.sin(angle) + KX * unit * np.sin(end_angle)) / count
    keep = (1.0 + 2.0 * np.cos(angle).sum(axis=0) + np.cos(end_angle)) / count
    shift = (lag[None, :] - lag[:, None]) % count
    ends = 2.0 * np.pi / count * (KX * lag % count)
    return slope[shift], keep[shift], np.cos(ends), np.sin(ends), KX * unit


def dot(a, b, dims):
    return lax.dot_general(a, b, (dims, ((), ())), preferred_element_type=F32)


def drag_kernel(level, area, wall_heat, u, v, c, heights, classes, fu, fv, us, vs, heating):
    rows, columns = u.shape
    lanes = min(512, columns)
    for r in range(0, rows, 16):
        for q in range(0, columns, lanes):
            at = (slice(r, r + 16), slice(q, q + lanes))
            kind = classes[at]
            density = jnp.full(kind.shape, area[0], F32)
            heat = jnp.full(kind.shape, wall_heat[0], F32)
            for k in range(1, area.shape[0]):
                match = kind == k
                density = jnp.where(match, area[k], density)
                heat = jnp.where(match, wall_heat[k], heat)
            inside = level[0] < heights[at]
            east, north = u[at].astype(F32), v[at].astype(F32)
            tracer = c[at].astype(F32)
            speed = jnp.sqrt(east * east + north * north + GUST_FLOOR)
            drag = 1.0 + jnp.where(inside, DRAG_STEP * density * speed, 0.0)
            inverse = 1.0 / drag
            east, north = east * inverse, north * inverse
            fu[at] = (east * tracer).astype(BF)
            fv[at] = (north * tracer).astype(BF)
            us[at] = east.astype(BF)
            vs[at] = north.astype(BF)
            heating[at] = jnp.where(inside, heat, 0.0)


def drag_fields(level, area, wall_heat, u, v, c, heights, classes):
    rows, columns = u.shape
    block = min(64, rows)
    small = pl.BlockSpec(memory_space=pltpu.SMEM)
    strip = pl.BlockSpec((block, columns), lambda i: (i, 0))
    shape = lambda dtype: jax.ShapeDtypeStruct((rows, columns), dtype)
    return pl.pallas_call(
        drag_kernel,
        grid=(rows // block,),
        in_specs=[small] * 3 + [strip] * 5,
        out_specs=[strip] * 5,
        out_shape=[shape(BF)] * 4 + [shape(F32)],
        compiler_params=pltpu.CompilerParams(vmem_limit_bytes=60 * 2**20),
        cost_estimate=pl.CostEstimate(
            flops=60 * rows * columns, bytes_accessed=26 * rows * columns, transcendentals=0
        ),
    )(level, area, wall_heat, u, v, c, heights, classes)


def per_device(tables, u_wind, v_wind, w_wind, scalar, heights, wall_class, wall_area, wall_heat):
    _, row_count, column_count = u_wind.shape
    strips = lax.axis_size("xy")
    groups = lax.axis_size("gz")
    level = lax.axis_index("gz")
    strip = lax.axis_index("xy")
    half, share, width = tables["half"], tables["share"], tables["width"]
    count_x = row_count * strips

    w_flat, c_flat = w_wind[0], scalar[0]
    up = [(i, i + 1) for i in range(groups - 1)]
    down = [(i + 1, i) for i in range(groups - 1)]
    flux_u, flux_v, u_bf, v_bf, heating = drag_fields(
        level.reshape(1), wall_area, wall_heat, u_wind[0], v_wind[0], c_flat, heights, wall_class
    )

    mn, nt, tn = ((1,), (0,)), ((1,), (1,)), ((0,), (0,))
    y_high, y_low = tables["y"]
    s_high, s_low = tables["y_slope"]
    exchange = partial(lax.all_to_all, axis_name="xy", split_axis=0, concat_axis=0, tiled=True)
    blocks = lambda t: t.reshape(strips, share, -1).astype(BF)
    east_spectra = blocks(dot(y_high, flux_u, nt))
    east_spectra, flux_v = lax.optimization_barrier((east_spectra, flux_v))
    z_east = exchange(east_spectra)
    north_spectra = blocks(dot(s_high, flux_v, nt))
    north_spectra, c_flat, w_flat, u_bf, v_bf = lax.optimization_barrier(
        (north_spectra, c_flat, w_flat, u_bf, v_bf)
    )
    z_north = exchange(north_spectra)
    c_below = lax.ppermute(c_flat, "gz", up)

    first_row = strip * row_count
    rows = lambda t: lax.dynamic_slice_in_dim(t, first_row, row_count, 1)
    basis = jnp.concatenate([rows(tables["basis"][0]), rows(tables["basis"][1])], axis=1)
    slope = jnp.concatenate([rows(tables["slope"][0]), rows(tables["slope"][1])], axis=1)
    low_modes = lambda table, field: dot(table, jnp.concatenate([field, field], axis=0), mn)
    w_modes = low_modes(basis, w_flat) * (1.0 / LEVEL_STEP)
    a_modes = low_modes(slope, u_bf) - w_modes
    b_modes = low_modes(basis, v_bf)

    def three(high, low, modes):
        m_high, m_low = split(modes)
        return dot(high, m_high, nt) + dot(high, m_low, nt) + dot(low, m_high, nt)

    rhs_part = three(y_high, y_low, a_modes) + three(s_high, s_low, b_modes)
    low_part = three(y_high, y_low, w_modes)
    got = exchange(blocks(jnp.concatenate([rhs_part, low_part], axis=1)))

    tracer = c_flat.astype(F32)
    flux = w_flat.astype(F32) * (tracer + c_below.astype(F32)) * (0.5 / LEVEL_STEP)
    flux_above = lax.ppermute(flux.astype(BF), "gz", down)

    sums = jnp.sum(got.astype(F32), axis=0)
    all_sums = lax.all_gather(sums, "gz", axis=0, tiled=False)
    wave_own = lax.dynamic_index_in_dim(
        jnp.asarray(tables["wave_y"], F32), strip, 0, keepdims=False
    )
    wave_x = jnp.asarray(tables["wave_x"], F32)
    coupling = 1.0 / (LEVEL_STEP * LEVEL_STEP)
    diagonal = -2.0 * coupling - (wave_x * wave_x)[None, :] - (wave_own * wave_own)[:, None]
    ratio = jnp.zeros_like(diagonal)
    reduced = jnp.zeros_like(diagonal)
    ratios, reduced_list = [], []
    for l in range(groups):
        rhs = all_sums[l, :, :width]
        if l + 1 < groups:
            rhs = rhs + all_sums[l + 1, :, width:]
        inverse = 1.0 / (diagonal - coupling * ratio)
        ratio = coupling * inverse
        reduced = (rhs - coupling * reduced) * inverse
        ratios.append(ratio)
        reduced_list.append(reduced)
    value = jnp.zeros_like(diagonal)
    own = jnp.zeros_like(diagonal)
    for l in reversed(range(groups)):
        value = reduced_list[l] - ratios[l] * value
        own = jnp.where(level == l, value, own)
    corner = own[2 * half : 2 * half + 2, 2 * BAND : 2 * BAND + 2]
    sign = np.array([[-1.0, 1.0], [1.0, -1.0]], np.float32)
    fixed = corner + sign * corner[::-1, ::-1]
    corner = jnp.where(strip == strips - 1, fixed, corner)
    own = lax.dynamic_update_slice(own, corner, (2 * half, 2 * BAND))
    synth_y = lax.dynamic_index_in_dim(
        jnp.asarray(tables["synth_y"], F32), strip, 0, keepdims=False
    )[:, None]
    own = own * (synth_y * jnp.asarray(tables["synth_x"], F32)[None, :] * tables["gain"])

    wide = lambda t: jnp.swapaxes(t, 0, 1).reshape(share, count_x)
    z_east, z_north = wide(z_east), wide(z_north)
    product = dot(z_east, tables["x_slope"], mn) + dot(z_north, tables["x_keep"], mn)
    ends = jnp.asarray(tables["ends"], F32)
    pe = z_east[2 * half : 2 * half + 2].astype(F32)
    pn = z_north[2 * half : 2 * half + 2].astype(F32)
    top = tables["top"]
    ec, es = jnp.sum(pe * ends[0], axis=1), jnp.sum(pe * ends[1], axis=1)
    nc, ns = jnp.sum(pn * ends[0], axis=1), jnp.sum(pn * ends[1], axis=1)
    cos_gain = (-top * ec + ns) / count_x
    sin_gain = (-top * es - nc) / count_x
    imag = cos_gain[:, None] * ends[0] + sin_gain[:, None] * ends[1]
    imag = jnp.where(strip == strips - 1, jnp.stack([-imag[1], imag[0]]), 0.0)
    product = lax.dynamic_update_slice(
        product, product[2 * half : 2 * half + 2] + imag, (2 * half, 0)
    )
    product = product * synth_y
    back = jnp.swapaxes(product.reshape(share, strips, row_count), 0, 1).astype(BF)
    returned = exchange(back).reshape(strips * share, row_count)
    solved = lax.all_gather(own.astype(BF), "xy", axis=0, tiled=True)

    pressed = dot(solved, y_high, tn) + dot(solved, y_low, tn)
    p_high, p_low = split(pressed)
    b_high, b_low = rows(tables["basis"][0]), rows(tables["basis"][1])
    pressure = dot(
        jnp.concatenate([b_high, b_low, b_high], axis=0),
        jnp.concatenate([p_high, p_high, p_low], axis=0),
        tn,
    ) * (1.0 / tables["gain"])
    vertical = flux_above.astype(F32) - flux
    tendency = (heating - dot(returned, y_high, tn) - vertical).astype(BF)
    return (tendency[None], pressure[None])


def solution(mesh):

    def whole(u_wind, *others):
        _, count_x, count_y = u_wind.shape
        strips = mesh.shape["xy"]
        half, share, y_table, y_slope, wave_y, synth_y = y_layout(strips, count_y)
        width, basis, slope, wave_x, synth_x = x_band(count_x)
        x_slope, x_keep, end_cos, end_sin, top = x_operators(count_x)
        tables = {
            "half": half,
            "share": share,
            "width": width,
            "y": split_np(y_table),
            "y_slope": split_np(y_slope),
            "wave_y": wave_y,
            "synth_y": synth_y,
            "basis": split_np(basis),
            "slope": split_np(slope),
            "wave_x": wave_x,
            "synth_x": synth_x,
            "gain": float(count_x),
            "x_slope": x_slope.astype(ml_dtypes.bfloat16),
            "x_keep": x_keep.astype(ml_dtypes.bfloat16),
            "ends": np.stack([end_cos, end_sin]),
            "top": top,
        }
        return jax.shard_map(
            partial(per_device, tables),
            mesh=mesh,
            in_specs=(P("gz", "xy", None),) * 4 + (P("xy", None),) * 2 + (P(), P()),
            out_specs=(P("gz", "xy", None), P("gz", "xy", None)),
            check_vma=False,
        )(u_wind, *others)

    return whole
```

```python
from functools import partial
import math

import jax
import jax.numpy as jnp
import ml_dtypes
import numpy as np
from jax import lax
from jax.experimental import pallas as pl
from jax.experimental.pallas import tpu as pltpu
from jax.sharding import PartitionSpec as P

KX = 640
KY = 640
BAND = 64

GRID_STEP = 2.5
LEVEL_STEP = 2.5
DRAG_STEP = 0.5
GUST_FLOOR = 0.25

BF = jnp.bfloat16
F32 = jnp.float32


def round_up(value, unit):
    return -(-value // unit) * unit


def split_np(table):
    high = table.astype(ml_dtypes.bfloat16)
    low = (table - high.astype(np.float64)).astype(ml_dtypes.bfloat16)
    return high, low


def split(array):
    high = lax.reduce_precision(array, exponent_bits=8, mantissa_bits=7)
    return high.astype(BF), (array - high).astype(BF)


def mode_rows(modes_c, modes_s, count):
    t = np.arange(count)
    cos_rows = np.cos(2.0 * np.pi / count * (np.outer(modes_c, t) % count))
    sin_rows = np.sin(2.0 * np.pi / count * (np.outer(modes_s, t) % count))
    return cos_rows, sin_rows


def y_layout(strips, count):
    half = KY // strips
    share = round_up(2 * half + 2, 8)
    table = np.zeros((strips, share, count))
    synth = np.zeros((strips, share))
    wave = np.zeros((strips, share))
    for d in range(strips):
        modes = np.arange(d * half, (d + 1) * half)
        table[d, :half], table[d, half : 2 * half] = mode_rows(modes, modes, count)
        wave[d, :half] = wave[d, half : 2 * half] = modes
        synth[d, : 2 * half] = 2.0 / count
    synth[0, 0] = 1.0 / count
    ends = np.array([KY])
    cos_end, sin_end = mode_rows(ends, ends, count)
    table[-1, 2 * half], table[-1, 2 * half + 1] = cos_end[0], sin_end[0]
    wave[-1, 2 * half : 2 * half + 2] = KY
    synth[-1, 2 * half : 2 * half + 2] = 1.0 / count
    wave *= 2.0 * np.pi / (count * GRID_STEP)
    slope = np.zeros((strips, share, count))
    slope[:, :half] = wave[:, :half, None] * table[:, half : 2 * half]
    slope[:, half : 2 * half] = -wave[:, half : 2 * half, None] * table[:, :half]
    slope[:, 2 * half] = wave[:, 2 * half, None] * table[:, 2 * half + 1]
    slope[:, 2 * half + 1] = -wave[:, 2 * half + 1, None] * table[:, 2 * half]
    flat = (strips * share, count)
    return half, share, table.reshape(flat), slope.reshape(flat), wave, synth


def x_band(count):
    width = round_up(2 * BAND + 2, 8)
    modes = np.arange(BAND)
    basis = np.zeros((width, count))
    basis[:BAND], basis[BAND : 2 * BAND] = mode_rows(modes, modes, count)
    ends = np.array([BAND])
    cos_end, sin_end = mode_rows(ends, ends, count)
    basis[2 * BAND], basis[2 * BAND + 1] = cos_end[0], sin_end[0]
    unit = 2.0 * np.pi / (count * GRID_STEP)
    wave = np.zeros(width)
    wave[:BAND] = wave[BAND : 2 * BAND] = modes * unit
    wave[2 * BAND : 2 * BAND + 2] = BAND * unit
    slope = np.zeros((width, count))
    slope[:BAND] = wave[:BAND, None] * basis[BAND : 2 * BAND]
    slope[BAND : 2 * BAND] = -wave[:BAND, None] * basis[:BAND]
    slope[2 * BAND] = wave[2 * BAND] * basis[2 * BAND + 1]
    slope[2 * BAND + 1] = -wave[2 * BAND] * basis[2 * BAND]
    synth = np.zeros(width)
    synth[: 2 * BAND] = 2.0 / count
    synth[0] = 1.0 / count
    synth[2 * BAND : 2 * BAND + 2] = 1.0 / count
    return width, basis, slope, wave, synth


def x_operators(count):
    modes = np.arange(1, KX)
    unit = 2.0 * np.pi / (count * GRID_STEP)
    lag = np.arange(count)
    angle = 2.0 * np.pi / count * (np.outer(modes, lag) % count)
    end_angle = 2.0 * np.pi / count * (KX * lag % count)
    slope = -(2.0 * (modes * unit) @ np.sin(angle) + KX * unit * np.sin(end_angle)) / count
    keep = (1.0 + 2.0 * np.cos(angle).sum(axis=0) + np.cos(end_angle)) / count
    shift = (lag[None, :] - lag[:, None]) % count
    ends = 2.0 * np.pi / count * (KX * lag % count)
    return slope[shift], keep[shift], np.cos(ends), np.sin(ends), KX * unit


def dot(a, b, dims):
    return lax.dot_general(a, b, (dims, ((), ())), preferred_element_type=F32)


def drag_kernel(level, area, wall_heat, u, v, c, heights, classes, fu, fv, us, vs, heating):
    rows, columns = u.shape
    lanes = min(512, columns)
    for r in range(0, rows, 16):
        for q in range(0, columns, lanes):
            at = (slice(r, r + 16), slice(q, q + lanes))
            kind = classes[at]
            density = jnp.full(kind.shape, area[0], F32)
            heat = jnp.full(kind.shape, wall_heat[0], F32)
            for k in range(1, area.shape[0]):
                match = kind == k
                density = jnp.where(match, area[k], density)
                heat = jnp.where(match, wall_heat[k], heat)
            inside = level[0] < heights[at]
            east, north = u[at].astype(F32), v[at].astype(F32)
            tracer = c[at].astype(F32)
            speed = jnp.sqrt(east * east + north * north + GUST_FLOOR)
            drag = 1.0 + jnp.where(inside, DRAG_STEP * density * speed, 0.0)
            inverse = 1.0 / drag
            east, north = east * inverse, north * inverse
            fu[at] = (east * tracer).astype(BF)
            fv[at] = (north * tracer).astype(BF)
            us[at] = east.astype(BF)
            vs[at] = north.astype(BF)
            heating[at] = jnp.where(inside, heat, 0.0)


def drag_fields(level, area, wall_heat, u, v, c, heights, classes):
    rows, columns = u.shape
    block = min(64, rows)
    small = pl.BlockSpec(memory_space=pltpu.SMEM)
    strip = pl.BlockSpec((block, columns), lambda i: (i, 0))
    shape = lambda dtype: jax.ShapeDtypeStruct((rows, columns), dtype)
    return pl.pallas_call(
        drag_kernel,
        grid=(rows // block,),
        in_specs=[small] * 3 + [strip] * 5,
        out_specs=[strip] * 5,
        out_shape=[shape(BF)] * 4 + [shape(F32)],
        compiler_params=pltpu.CompilerParams(vmem_limit_bytes=60 * 2**20),
        cost_estimate=pl.CostEstimate(
            flops=60 * rows * columns, bytes_accessed=26 * rows * columns, transcendentals=0
        ),
    )(level, area, wall_heat, u, v, c, heights, classes)


def per_device(tables, u_wind, v_wind, w_wind, scalar, heights, wall_class, wall_area, wall_heat):
    _, row_count, column_count = u_wind.shape
    strips = lax.axis_size("xy")
    groups = lax.axis_size("gz")
    level = lax.axis_index("gz")
    strip = lax.axis_index("xy")
    half, share, width = tables["half"], tables["share"], tables["width"]
    count_x = row_count * strips

    w_flat, c_flat = w_wind[0], scalar[0]
    up = [(i, i + 1) for i in range(groups - 1)]
    down = [(i + 1, i) for i in range(groups - 1)]
    flux_u, flux_v, u_bf, v_bf, heating = drag_fields(
        level.reshape(1), wall_area, wall_heat, u_wind[0], v_wind[0], c_flat, heights, wall_class
    )

    mn, nt, tn = ((1,), (0,)), ((1,), (1,)), ((0,), (0,))
    y_high, y_low = tables["y"]
    s_high, s_low = tables["y_slope"]
    exchange = partial(lax.all_to_all, axis_name="xy", split_axis=0, concat_axis=0, tiled=True)
    blocks = lambda t: t.reshape(strips, share, -1).astype(BF)
    east_spectra = blocks(dot(y_high, flux_u, nt))
    north_spectra = blocks(dot(s_high, flux_v, nt))
    spectra = jnp.concatenate([east_spectra, north_spectra], axis=-1)
    spectra, c_flat, w_flat, u_bf, v_bf = lax.optimization_barrier(
        (spectra, c_flat, w_flat, u_bf, v_bf)
    )
    spectra = exchange(spectra)
    z_east, z_north = spectra[..., :row_count], spectra[..., row_count:]
    c_below = lax.ppermute(c_flat, "gz", up)

    first_row = strip * row_count
    rows = lambda t: lax.dynamic_slice_in_dim(t, first_row, row_count, 1)
    basis = jnp.concatenate([rows(tables["basis"][0]), rows(tables["basis"][1])], axis=1)
    slope = jnp.concatenate([rows(tables["slope"][0]), rows(tables["slope"][1])], axis=1)
    low_modes = lambda table, field: dot(table, jnp.concatenate([field, field], axis=0), mn)
    w_modes = low_modes(basis, w_flat) * (1.0 / LEVEL_STEP)
    a_modes = low_modes(slope, u_bf) - w_modes
    b_modes = low_modes(basis, v_bf)

    def three(high, low, modes):
        m_high, m_low = split(modes)
        return dot(high, m_high, nt) + dot(high, m_low, nt) + dot(low, m_high, nt)

    rhs_part = three(y_high, y_low, a_modes) + three(s_high, s_low, b_modes)
    low_part = three(y_high, y_low, w_modes)
    got = exchange(blocks(jnp.concatenate([rhs_part, low_part], axis=1)))

    tracer = c_flat.astype(F32)
    flux = w_flat.astype(F32) * (tracer + c_below.astype(F32)) * (0.5 / LEVEL_STEP)
    flux_above = lax.ppermute(flux.astype(BF), "gz", down)

    sums = jnp.sum(got.astype(F32), axis=0)
    all_sums = lax.all_gather(sums, "gz", axis=0, tiled=False)
    wave_own = lax.dynamic_index_in_dim(
        jnp.asarray(tables["wave_y"], F32), strip, 0, keepdims=False
    )
    wave_x = jnp.asarray(tables["wave_x"], F32)
    coupling = 1.0 / (LEVEL_STEP * LEVEL_STEP)
    diagonal = -2.0 * coupling - (wave_x * wave_x)[None, :] - (wave_own * wave_own)[:, None]
    ratio = jnp.zeros_like(diagonal)
    reduced = jnp.zeros_like(diagonal)
    ratios, reduced_list = [], []
    for l in range(groups):
        rhs = all_sums[l, :, :width]
        if l + 1 < groups:
            rhs = rhs + all_sums[l + 1, :, width:]
        inverse = 1.0 / (diagonal - coupling * ratio)
        ratio = coupling * inverse
        reduced = (rhs - coupling * reduced) * inverse
        ratios.append(ratio)
        reduced_list.append(reduced)
    value = jnp.zeros_like(diagonal)
    own = jnp.zeros_like(diagonal)
    for l in reversed(range(groups)):
        value = reduced_list[l] - ratios[l] * value
        own = jnp.where(level == l, value, own)
    corner = own[2 * half : 2 * half + 2, 2 * BAND : 2 * BAND + 2]
    sign = np.array([[-1.0, 1.0], [1.0, -1.0]], np.float32)
    fixed = corner + sign * corner[::-1, ::-1]
    corner = jnp.where(strip == strips - 1, fixed, corner)
    own = lax.dynamic_update_slice(own, corner, (2 * half, 2 * BAND))
    synth_y = lax.dynamic_index_in_dim(
        jnp.asarray(tables["synth_y"], F32), strip, 0, keepdims=False
    )[:, None]
    own = own * (synth_y * jnp.asarray(tables["synth_x"], F32)[None, :] * tables["gain"])

    wide = lambda t: jnp.swapaxes(t, 0, 1).reshape(share, count_x)
    z_east, z_north = wide(z_east), wide(z_north)
    product = dot(z_east, tables["x_slope"], mn) + dot(z_north, tables["x_keep"], mn)
    ends = jnp.asarray(tables["ends"], F32)
    pe = z_east[2 * half : 2 * half + 2].astype(F32)
    pn = z_north[2 * half : 2 * half + 2].astype(F32)
    top = tables["top"]
    ec, es = jnp.sum(pe * ends[0], axis=1), jnp.sum(pe * ends[1], axis=1)
    nc, ns = jnp.sum(pn * ends[0], axis=1), jnp.sum(pn * ends[1], axis=1)
    cos_gain = (-top * ec + ns) / count_x
    sin_gain = (-top * es - nc) / count_x
    imag = cos_gain[:, None] * ends[0] + sin_gain[:, None] * ends[1]
    imag = jnp.where(strip == strips - 1, jnp.stack([-imag[1], imag[0]]), 0.0)
    product = lax.dynamic_update_slice(
        product, product[2 * half : 2 * half + 2] + imag, (2 * half, 0)
    )
    product = product * synth_y
    back = jnp.swapaxes(product.reshape(share, strips, row_count), 0, 1).astype(BF)
    returned = exchange(back).reshape(strips * share, row_count)
    solved = lax.all_gather(own.astype(BF), "xy", axis=0, tiled=True)

    pressed = dot(solved, y_high, tn) + dot(solved, y_low, tn)
    p_high, p_low = split(pressed)
    b_high, b_low = rows(tables["basis"][0]), rows(tables["basis"][1])
    pressure = dot(
        jnp.concatenate([b_high, b_low, b_high], axis=0),
        jnp.concatenate([p_high, p_high, p_low], axis=0),
        tn,
    ) * (1.0 / tables["gain"])
    vertical = flux_above.astype(F32) - flux
    tendency = (heating - dot(returned, y_high, tn) - vertical).astype(BF)
    return (tendency[None], pressure[None])


def solution(mesh):

    def whole(u_wind, *others):
        _, count_x, count_y = u_wind.shape
        strips = mesh.shape["xy"]
        half, share, y_table, y_slope, wave_y, synth_y = y_layout(strips, count_y)
        width, basis, slope, wave_x, synth_x = x_band(count_x)
        x_slope, x_keep, end_cos, end_sin, top = x_operators(count_x)
        tables = {
            "half": half,
            "share": share,
            "width": width,
            "y": split_np(y_table),
            "y_slope": split_np(y_slope),
            "wave_y": wave_y,
            "synth_y": synth_y,
            "basis": split_np(basis),
            "slope": split_np(slope),
            "wave_x": wave_x,
            "synth_x": synth_x,
            "gain": float(count_x),
            "x_slope": x_slope.astype(ml_dtypes.bfloat16),
            "x_keep": x_keep.astype(ml_dtypes.bfloat16),
            "ends": np.stack([end_cos, end_sin]),
            "top": top,
        }
        return jax.shard_map(
            partial(per_device, tables),
            mesh=mesh,
            in_specs=(P("gz", "xy", None),) * 4 + (P("xy", None),) * 2 + (P(), P()),
            out_specs=(P("gz", "xy", None), P("gz", "xy", None)),
            check_vma=False,
        )(u_wind, *others)

    return whole
```
